32 devices in a mesh: groups: 2 (over y), tiles: 8 (over z, x), comp: 2 (over core).
Axes of the slice: x: 2, y: 2, z: 4, core: 2. Of those that a mesh axis runs over, the one named last changes fastest.
Arguments:
- state_field: bfloat16 [2, 384, 16384], P('comp', None, ('groups', 'tiles')), parts along dimension 2, may hold values from -6 to 6
- cotangent: bfloat16 [2, 384, 16384], P('comp', None, ('groups', 'tiles')), parts along dimension 2, may hold values from -6 to 6
- w_in: bfloat16 [2, 384, 1536], P('comp'), may hold values from -0.3125 to 0.3125
- w_out: bfloat16 [2, 1536, 384], P('comp'), may hold values from -0.15625 to 0.15625
- norm_gain: float32 [2, 384], P('comp'), may hold values from 0.5 to 1.5
- export_weight: bfloat16 [2, 8, 384], P('comp'), may hold values from -0.3125 to 0.3125
- lift_weight: float32 [2, 384, 8], P('comp'), may hold values from -2 to 2
- wet_mask: int32 [16384], P(('groups', 'tiles')), parts along dimension 0, may hold values 0 or 1
- remap_tile: int32 [2, 512, 1], P('comp', 'tiles'), may hold values from 0 to 7; in each aligned block of 64 rows (0 to 63, 64 to 127, ..., all dimensions but the last counted through in order) at most 16 rows name the same one
- source_block: int32 [2, 512], P('comp', 'tiles'), may hold values from 0 to 7
- target_block: int32 [2, 512], P('comp', 'tiles'), may hold values from 0 to 7
- slot_alive: int32 [2, 512], P('comp', 'tiles'), may hold values 0 or 1
- remap_weights: bfloat16 [2, 512, 128, 128], P('comp', 'tiles'), may hold values from -0.5 to 0.5
Outputs:
- grad_state: float32 [2, 384, 16384], P('comp', None, ('groups', 'tiles')), parts along dimension 2
- grad_w_in: float32 [4, 384, 1536], P(('groups', 'comp')), parts along dimension 0
- grad_w_out: float32 [4, 1536, 384], P(('groups', 'comp')), parts along dimension 0
- grad_gain: float32 [4, 384], P(('groups', 'comp')), parts along dimension 0
- grad_export: float32 [4, 8, 384], P(('groups', 'comp')), parts along dimension 0
- grad_lift: float32 [4, 384, 8], P(('groups', 'comp')), parts along dimension 0
The draws below stay inside these ranges and needn't reach their ends.
There are 2 independent parts, one for each index of `groups`. The reference program is written for one: setup_inputs(seed, part) draws one part's arguments, and reference() takes and returns one part's arrays. A program takes and returns all parts, laid end to end along the dimension named above; an argument that names none is the same for every part. Nothing has to cross between parts.
Inputs may be any that keep to these rules, and one draw needn't show every extreme that they name: `remap_tile`: at most 16 slots of one tile of a component name the same target tile, and some tile reaches that bound.
All inputs are finite; a program needn't handle non-finite values. No bound on the sum of `wet_mask` or of `slot_alive` on one device may be relied on, other than what follows from the above.
Results may differ from the reference program's by a relative error of at most 0.0057.
Values may be sent and summed in bfloat16 or wider, within the bound.
A program may use at most 64 MiB of HBM per device.

```python
import math
from functools import partial
import jax
import jax.numpy as jnp
import numpy as np
from jax import lax

C = 384
HID = 1536
K = 8
BLK = 128
CELLS = 1024
BLOCKS = 8
SLOTS = 64
CAP = 16
NP = 8192
N_TILES = 8


def with_ends(drawn, rng, low, high):
    longest = drawn.shape.index(max(drawn.shape))
    spots = []
    for shift in (0, 1):
        where = [jax.random.randint(jax.random.fold_in(rng, axis), (), 0, length) for axis, length in enumerate(drawn.shape)]
        where[longest] = (where[longest] + shift) % drawn.shape[longest]
        spots.append(tuple(where))
    return drawn.at[spots[0]].set(low).at[spots[1]].set(high)


def levels(stream_key, shape, cuts, smallest, high):
    loudness = 1.0
    for axis_at, shards_of in cuts:
        heights = jax.random.uniform(jax.random.fold_in(jax.random.fold_in(stream_key, 6), axis_at), (shards_of,), jnp.float32, smallest / len(cuts), high / len(cuts))
        loudness = loudness * jnp.repeat(jnp.exp(heights), shape[axis_at] // shards_of).reshape((-1,) + (1,) * (len(shape) - 1 - axis_at))
    return loudness


def assign_block(key, own, number, rows, number_of, top, limit, lean):
    ranking = jax.random.permutation(key, number_of)
    packed, usual = shares(number_of, rows * top, limit, lean, True), shares(number_of, rows * top, limit, lean, False)
    places = jnp.arange(number_of)

    def named(lengths, turn):
        used = int((lengths > 0).sum())
        fixed = max(1, used // 4)
        shifted = fixed + (places - fixed + turn * (used - fixed)) % max(1, number_of - fixed)
        return jnp.zeros((number_of,), jnp.int32).at[ranking[jnp.where(places < fixed, places, shifted)]].set(jnp.asarray(lengths, jnp.int32))

    lengths = jnp.where(number % 4 == 0, named(packed, number // 4), named(usual, number - number // 4 - 1))
    mixed = jax.random.permutation(jax.random.fold_in(own, 3), number_of)
    source_of, taker = mixed[0:number_of // 2 * 2:2], mixed[1:number_of // 2 * 2:2]
    room = jnp.minimum(lengths[source_of] - 1, limit - lengths[taker]) // 2
    room = jnp.where((source_of == ranking[0]) | (taker == ranking[0]) | (lengths[taker] == 0), 0, jnp.maximum(room, 0))
    shifted = jax.random.randint(jax.random.fold_in(own, 4), (number_of // 2,), 0, 1 << 20) % (room + 1)
    lengths = lengths.at[source_of].add(-shifted).at[taker].add(shifted)
    items = jnp.searchsorted(jnp.cumsum(lengths), jnp.arange(rows * top), side="right").astype(jnp.int32)
    table = items.reshape(top, rows).T
    table = table[jax.random.permutation(jax.random.fold_in(own, 1), rows)]
    turn = jax.random.randint(jax.random.fold_in(own, 2), (rows, 1), 0, top)
    return jnp.take_along_axis(table, (jnp.arange(top)[None, :] + turn) % top, axis=1)


def shares(amount, total, reach, skew, full):
    portions = [(1 << 20) // math.isqrt(grade ** skew) + 1 for grade in range(1, amount + 1)]
    largest = reach if full else min(reach, max(-(-total // amount), total * portions[0] // sum(portions)))
    least = 1 if total - largest >= amount - 1 else 0
    counts, surplus = [largest] + [least] * (amount - 1), total - largest - least * (amount - 1)
    while surplus > 0:
        movable = [i for i in range(1, amount) if counts[i] < largest] or [i for i in range(1, amount) if counts[i] < reach]
        mass, remaining = sum([portions[i] for i in movable]), surplus
        for i in movable:
            extra = min(reach - counts[i], max(1, remaining * portions[i] // mass), surplus)
            counts[i] = counts[i] + extra
            surplus = surplus - extra
    return np.array(counts)


def centred(rng, extent, scale, bound, shards=(), kind=jnp.bfloat16):
    drawn = scale * jax.random.normal(rng, extent, jnp.float32)
    if shards:
        drawn = drawn * levels(rng, extent, shards, -0.22, 0.18)
    return jnp.clip(drawn, -bound, bound).astype(kind)


def setup_inputs(seed: int = 0, part: int = 0) -> dict:
    seeds = jax.random.split(jax.random.key(seed), 14)
    part_keys = jax.random.split(jax.random.fold_in(seeds[13], part), 14)
    state_field = centred(part_keys[0], (2, C, NP), 1.0, 6.0, ((0, 2), (2, 8)))
    cotangent = centred(part_keys[1], (2, C, NP), 1.0, 6.0, ((0, 2), (2, 8)))
    w_in = centred(seeds[2], (2, C, HID), C ** -0.5, 0.3125, ((0, 2),))
    w_out = centred(seeds[3], (2, HID, C), HID ** -0.5, 0.15625, ((0, 2),))
    norm_gain = jnp.clip(1.0 + 0.1 * jax.random.normal(seeds[4], (2, C), jnp.float32), 0.5, 1.5)
    export_weight = centred(seeds[5], (2, K, C), C ** -0.5, 0.3125, ((0, 2),))
    lift_weight = centred(seeds[6], (2, C, K), K ** -0.5, 2.0, ((0, 2),), jnp.float32)
    wet_mask = with_ends((jax.random.randint(part_keys[7], (NP,), 0, 10) < 7).astype(jnp.int32), jax.random.fold_in(part_keys[7], 1), 0, 1)
    remap_tile_keys = jax.random.split(jax.random.fold_in(seeds[8], 1), 2 * (N_TILES * SLOTS) // SLOTS)
    remap_tile_turns = jax.random.permutation(jax.random.fold_in(seeds[8], 3), 2 * (N_TILES * SLOTS) // SLOTS)
    remap_tile = jax.vmap(lambda own, number: assign_block(jax.random.fold_in(seeds[8], 2), own, number, SLOTS, N_TILES, 1, CAP, 2))(remap_tile_keys, remap_tile_turns).reshape((2, N_TILES * SLOTS, 1))
    source_block = with_ends(jax.random.randint(seeds[9], (2, N_TILES * SLOTS), 0, BLOCKS), jax.random.fold_in(seeds[9], 1), 0, BLOCKS - 1).astype(jnp.int32)
    target_block = with_ends(jax.random.randint(seeds[10], (2, N_TILES * SLOTS), 0, BLOCKS), jax.random.fold_in(seeds[10], 1), 0, BLOCKS - 1).astype(jnp.int32)
    slot_alive = with_ends((jax.random.randint(seeds[11], (2, N_TILES * SLOTS), 0, 4) < 3).astype(jnp.int32), jax.random.fold_in(seeds[11], 1), 0, 1)
    remap_weights = centred(seeds[12], (2, N_TILES * SLOTS, BLK, BLK), BLK ** -0.5, 0.5, ((0, 2), (1, 8)))
    return {"state_field": state_field, "cotangent": cotangent, "w_in": w_in, "w_out": w_out, "norm_gain": norm_gain, "export_weight": export_weight, "lift_weight": lift_weight, "wet_mask": wet_mask, "remap_tile": remap_tile, "source_block": source_block, "target_block": target_block, "slot_alive": slot_alive, "remap_weights": remap_weights}


norm_eps = 1e-05
highest = lax.Precision.HIGHEST

def gelu_parts(hidden):
    inner = 0.7978845608 * (hidden + 0.044715 * hidden * hidden * hidden)
    tanh_inner = jnp.tanh(inner)
    gelu_value = 0.5 * hidden * (1.0 + tanh_inner)
    gelu_slope = 0.5 * (1.0 + tanh_inner) + 0.5 * hidden * (1.0 - tanh_inner * tanh_inner) * 0.7978845608 * (1.0 + 0.134145 * hidden * hidden)
    return (gelu_value, gelu_slope)

def slot_indices(remap_tile, source_block, target_block):
    owner = jnp.arange(N_TILES * SLOTS, dtype=jnp.int32) // SLOTS
    source_index = (owner * BLOCKS + source_block.astype(jnp.int32)).astype(jnp.int32)
    target_index = (remap_tile[:, 0].astype(jnp.int32) * BLOCKS + target_block.astype(jnp.int32)).astype(jnp.int32)
    return (source_index, target_index)

def remap_forward(exported, weights, source_index, target_index, alive):
    block_rows = exported.reshape(K, N_TILES * BLOCKS, BLK)
    picked = jnp.take(block_rows, source_index, axis=1).astype(jnp.float32)
    products = jnp.einsum('kjp,jqp->jkq', picked, weights.astype(jnp.float32), precision=highest)
    products = products * alive[:, None, None]
    summed = jax.ops.segment_sum(products, target_index, num_segments=N_TILES * BLOCKS)
    return jnp.transpose(summed, (1, 0, 2)).reshape(K, NP)

def remap_adjoint(d_forcing, weights, source_index, target_index, alive):
    block_rows = d_forcing.reshape(K, N_TILES * BLOCKS, BLK)
    picked = jnp.take(block_rows, target_index, axis=1).astype(jnp.float32)
    products = jnp.einsum('kjq,jqp->jkp', picked, weights.astype(jnp.float32), precision=highest)
    products = products * alive[:, None, None]
    summed = jax.ops.segment_sum(products, source_index, num_segments=N_TILES * BLOCKS)
    return jnp.transpose(summed, (1, 0, 2)).reshape(K, NP)

def tile_backward(pieces, w_in, w_out, norm_gain, lift_weight):
    state_tile, forcing_tile, cotangent_tile, wet_tile = pieces
    summed_in = state_tile.astype(jnp.float32) + jnp.dot(lift_weight, forcing_tile, precision=highest, preferred_element_type=jnp.float32)
    centre = summed_in - lax.optimization_barrier(jnp.mean(summed_in, axis=0, keepdims=True))
    variance = lax.optimization_barrier(jnp.mean(centre * centre, axis=0, keepdims=True))
    inv_std = 1.0 / jnp.sqrt(variance + norm_eps)
    normed = centre * inv_std
    scaled = (norm_gain[:, None] * normed).astype(jnp.bfloat16)
    hidden = jnp.dot(w_in.T, scaled, preferred_element_type=jnp.float32)
    gelu_value, gelu_slope = gelu_parts(hidden)
    active = gelu_value.astype(jnp.bfloat16)
    masked = jnp.where(wet_tile[None, :] > 0, cotangent_tile, jnp.zeros_like(cotangent_tile))
    d_active = jnp.dot(w_out, masked, preferred_element_type=jnp.float32)
    g_out = jnp.dot(active, masked.T, preferred_element_type=jnp.float32)
    d_hidden = (d_active * gelu_slope).astype(jnp.bfloat16)
    g_in = jnp.dot(scaled, d_hidden.T, preferred_element_type=jnp.float32)
    d_scaled = jnp.dot(w_in, d_hidden, preferred_element_type=jnp.float32)
    g_gain = lax.optimization_barrier(jnp.sum(d_scaled * normed, axis=1))
    weighted = d_scaled * norm_gain[:, None]
    d_summed = inv_std * (weighted - lax.optimization_barrier(jnp.mean(weighted, axis=0, keepdims=True)) - normed * lax.optimization_barrier(jnp.mean(weighted * normed, axis=0, keepdims=True))) + masked.astype(jnp.float32)
    g_lift = jnp.dot(d_summed, forcing_tile.T, precision=highest, preferred_element_type=jnp.float32)
    d_forcing = jnp.dot(lift_weight.T, d_summed, precision=highest, preferred_element_type=jnp.float32).astype(jnp.bfloat16)
    return (d_summed, d_forcing, g_in, g_out, g_gain, g_lift)

def split_tiles(field):
    return jnp.transpose(field.reshape(field.shape[0], N_TILES, CELLS), (1, 0, 2))

def join_tiles(field):
    return jnp.transpose(field, (1, 0, 2)).reshape(field.shape[1], NP)

def reference(state_field, cotangent, w_in, w_out, norm_gain, export_weight, lift_weight, wet_mask, remap_tile, source_block, target_block, slot_alive, remap_weights):
    indices = [slot_indices(remap_tile[comp_index], source_block[comp_index], target_block[comp_index]) for comp_index in range(2)]
    alive = [slot_alive[comp_index].astype(jnp.float32) for comp_index in range(2)]
    exported = [jnp.dot(export_weight[comp_index], state_field[comp_index], preferred_element_type=jnp.float32).astype(jnp.bfloat16) for comp_index in range(2)]
    forcing = []
    for comp_index in range(2):
        other = 1 - comp_index
        forcing.append(remap_forward(exported[other], remap_weights[other], indices[other][0], indices[other][1], alive[other]))
    d_summed_all = []
    d_forcing_all = []
    grads_in = []
    grads_out = []
    grads_gain = []
    grads_lift = []
    for comp_index in range(2):
        if comp_index == 1:
            wet_field = wet_mask
        else:
            wet_field = jnp.ones_like(wet_mask)
        pieces = (split_tiles(state_field[comp_index]), split_tiles(forcing[comp_index]), split_tiles(cotangent[comp_index]), wet_field.reshape(N_TILES, CELLS))
        runner = partial(tile_backward, w_in=w_in[comp_index], w_out=w_out[comp_index], norm_gain=norm_gain[comp_index], lift_weight=lift_weight[comp_index])
        d_summed, d_forcing, g_in, g_out, g_gain, g_lift = lax.map(runner, pieces)
        d_summed_all.append(join_tiles(d_summed))
        d_forcing_all.append(join_tiles(d_forcing))
        grads_in.append(lax.optimization_barrier(jnp.sum(g_in, axis=0)))
        grads_out.append(lax.optimization_barrier(jnp.sum(g_out, axis=0)))
        grads_gain.append(lax.optimization_barrier(jnp.sum(g_gain, axis=0)))
        grads_lift.append(lax.optimization_barrier(jnp.sum(g_lift, axis=0)))
    grads_state = []
    grads_export = []
    for comp_index in range(2):
        other = 1 - comp_index
        d_exported = remap_adjoint(d_forcing_all[other], remap_weights[comp_index], indices[comp_index][0], indices[comp_index][1], alive[comp_index]).astype(jnp.bfloat16)
        grads_export.append(jnp.dot(d_exported, state_field[comp_index].T, preferred_element_type=jnp.float32))
        grads_state.append(d_summed_all[comp_index] + jnp.dot(export_weight[comp_index].T, d_exported, preferred_element_type=jnp.float32))
    return (jnp.stack(grads_state), jnp.stack(grads_in), jnp.stack(grads_out), jnp.stack(grads_gain), jnp.stack(grads_export), jnp.stack(grads_lift))
```

```python
import functools

import jax
import jax.numpy as jnp
from jax import lax
from jax.experimental import pallas as pl
from jax.experimental.pallas import tpu as pltpu
from jax.sharding import PartitionSpec as P

norm_eps = 1e-05
highest = lax.Precision.HIGHEST


def swapped(value, axis, distance):
    mask = 2**distance
    pairs = [(source, source ^ mask) for source in range(lax.axis_size(axis))]
    return lax.ppermute(value, axis, pairs)


def gelu_parts(hidden):
    inner = 0.7978845608 * (hidden + 0.044715 * hidden * hidden * hidden)
    tanh_inner = jnp.tanh(inner)
    gelu_value = 0.5 * hidden * (1.0 + tanh_inner)
    gelu_slope = 0.5 * (1.0 + tanh_inner) + 0.5 * hidden * (
        1.0 - tanh_inner * tanh_inner
    ) * 0.7978845608 * (1.0 + 0.134145 * hidden * hidden)
    return (gelu_value, gelu_slope)


def slots_across_tiles(values, block_ids):
    return (
        lax.all_to_all(values, "tiles", split_axis=0, concat_axis=0, tiled=True),
        lax.all_to_all(block_ids, "tiles", split_axis=0, concat_axis=0, tiled=True),
    )


def slots_across_comp(values, block_ids):
    return swapped((values, block_ids), "comp", 0)


def adjoint_across_tiles(values):
    return lax.all_to_all(values, "tiles", split_axis=0, concat_axis=0, tiled=True)


def adjoint_across_comp(values):
    return swapped(values, "comp", 0)


def general_body(
    state_field,
    cotangent,
    w_in,
    w_out,
    norm_gain,
    export_weight,
    lift_weight,
    wet_mask,
    remap_tile,
    source_block,
    target_block,
    slot_alive,
    remap_weights,
):
    tile_count = lax.axis_size("tiles")
    state_local = state_field[0]
    cotangent_local = cotangent[0]
    w_in_local = w_in[0]
    w_out_local = w_out[0]
    gain_local = norm_gain[0]
    export_local = export_weight[0]
    lift_local = lift_weight[0]
    weights_local = remap_weights[0]
    targets = remap_tile[0, :, 0]
    source_local = source_block[0]
    target_local = target_block[0]
    alive_local = slot_alive[0].astype(jnp.float32)
    channels, cell_count = state_local.shape
    field_count = export_local.shape[0]
    block_width = weights_local.shape[-1]
    block_count = cell_count // block_width
    slot_count = weights_local.shape[0]
    capacity = max(2, 2 * slot_count // tile_count)
    spot_count = tile_count * capacity
    exported = jnp.dot(export_local, state_local, preferred_element_type=jnp.float32).astype(
        jnp.bfloat16
    )
    pick_source = source_local[:, None] == jnp.arange(block_count, dtype=jnp.int32)[None, :]
    source_rows = jnp.einsum(
        "lb,kbp->lkp",
        pick_source.astype(jnp.bfloat16),
        exported.reshape(field_count, block_count, block_width),
        preferred_element_type=jnp.float32,
    ).astype(jnp.bfloat16)
    products = (
        jnp.einsum("lkp,lqp->lkq", source_rows, weights_local, preferred_element_type=jnp.float32)
        * alive_local[:, None, None]
    )
    to_tile = (targets[:, None] == jnp.arange(tile_count, dtype=jnp.int32)[None, :]).astype(
        jnp.int32
    )
    earlier = jnp.cumsum(to_tile, axis=0) - to_tile
    slot_rank = jnp.sum(earlier * to_tile, axis=1)
    position = targets * capacity + slot_rank
    placing = position[None, :] == jnp.arange(spot_count, dtype=jnp.int32)[:, None]
    outgoing = jnp.einsum("sl,lkq->skq", placing.astype(jnp.float32), products, precision=highest)
    outgoing_ids = jnp.sum(placing.astype(jnp.int32) * target_local[None, :], axis=1)
    middle, middle_ids = slots_across_comp(outgoing, outgoing_ids)
    incoming, incoming_ids = slots_across_tiles(middle, middle_ids)
    pick_target = incoming_ids[:, None] == jnp.arange(block_count, dtype=jnp.int32)[None, :]
    forcing = jnp.einsum(
        "sb,skq->kbq", pick_target.astype(jnp.float32), incoming, precision=highest
    ).reshape(field_count, cell_count)
    summed_in = state_local.astype(jnp.float32) + jnp.dot(
        lift_local, forcing, precision=highest, preferred_element_type=jnp.float32
    )
    centre = summed_in - jnp.mean(summed_in, axis=0, keepdims=True)
    variance = jnp.mean(centre * centre, axis=0, keepdims=True)
    inv_std = 1.0 / jnp.sqrt(variance + norm_eps)
    normed = centre * inv_std
    scaled = (gain_local[:, None] * normed).astype(jnp.bfloat16)
    hidden = jnp.einsum("ch,cp->hp", w_in_local, scaled, preferred_element_type=jnp.float32)
    gelu_value, gelu_slope = gelu_parts(hidden)
    active = gelu_value.astype(jnp.bfloat16)
    is_ocean = lax.axis_index("comp") == 1
    wet_factor = jnp.where(is_ocean, wet_mask, jnp.ones_like(wet_mask))
    masked = jnp.where(wet_factor[None, :] > 0, cotangent_local, jnp.zeros_like(cotangent_local))
    d_active = jnp.dot(w_out_local, masked, preferred_element_type=jnp.float32)
    g_out = jnp.einsum("hp,cp->hc", active, masked, preferred_element_type=jnp.float32)
    d_hidden = (d_active * gelu_slope).astype(jnp.bfloat16)
    g_in = jnp.einsum("cp,hp->ch", scaled, d_hidden, preferred_element_type=jnp.float32)
    d_scaled = jnp.dot(w_in_local, d_hidden, preferred_element_type=jnp.float32)
    g_gain = jnp.sum(d_scaled * normed, axis=1)
    weighted = d_scaled * gain_local[:, None]
    d_summed = inv_std * (
        weighted
        - jnp.mean(weighted, axis=0, keepdims=True)
        - normed * jnp.mean(weighted * normed, axis=0, keepdims=True)
    ) + masked.astype(jnp.float32)
    g_lift = jnp.einsum(
        "cp,kp->ck", d_summed, forcing, precision=highest, preferred_element_type=jnp.float32
    )
    d_forcing = jnp.einsum(
        "ck,cp->kp", lift_local, d_summed, precision=highest, preferred_element_type=jnp.float32
    ).astype(jnp.bfloat16)
    returning = jnp.einsum(
        "sb,kbq->skq",
        pick_target.astype(jnp.bfloat16),
        d_forcing.reshape(field_count, block_count, block_width),
        preferred_element_type=jnp.float32,
    ).astype(jnp.bfloat16)
    returned = adjoint_across_comp(adjoint_across_tiles(returning))
    slot_force = jnp.einsum(
        "sl,skq->lkq", placing.astype(jnp.bfloat16), returned, preferred_element_type=jnp.float32
    ).astype(jnp.bfloat16)
    pulled = (
        jnp.einsum("lkq,lqp->lkp", slot_force, weights_local, preferred_element_type=jnp.float32)
        * alive_local[:, None, None]
    )
    d_exported = (
        jnp.einsum("lb,lkp->kbp", pick_source.astype(jnp.float32), pulled, precision=highest)
        .reshape(field_count, cell_count)
        .astype(jnp.bfloat16)
    )
    g_export = jnp.einsum("kp,cp->kc", d_exported, state_local, preferred_element_type=jnp.float32)
    grad_local = d_summed + jnp.einsum(
        "kc,kp->cp", export_local, d_exported, preferred_element_type=jnp.float32
    )
    g_in, g_out, g_gain, g_export, g_lift = lax.psum(
        (g_in, g_out, g_gain, g_export, g_lift), "tiles"
    )
    return (grad_local[None], g_in[None], g_out[None], g_gain[None], g_export[None], g_lift[None])


MESH = pl.DeviceIdType.MESH
SUB = 2
NT = (((1,), (1,)), ((), ()))


def ring_place(tile, count):
    row, column = lax.div(tile, 2), lax.rem(tile, 2)
    return jnp.where(column == 0, row, count - 1 - row)


def ring_tile(place, count):
    return jnp.where(place < count // 2, 2 * place, 2 * (count - 1 - place) + 1)


def fused_kernel(
    count,
    spots_ref,
    coef_ref,
    partial_ref,
    state_ref,
    cot_ref,
    keep_ref,
    w_in_ref,
    w_out_ref,
    gain_ref,
    lift_ref,
    lift_t_ref,
    export_t_ref,
    weights_ref,
    grads_ref,
    small_ref,
    gs_ref,
    force_recv,
    w_in_t,
    masked,
    d_active,
    scaled,
    normed,
    inv_std,
    forcing,
    act,
    d_hidden,
    d_scaled,
    own,
    first,
    ring,
    df_send,
    df_recv,
    lower,
    blocks,
    small_send,
    small_recv,
    f_send,
    f_recv,
    a_send,
    a_recv,
    s_send,
    s_recv,
    rs_send,
    rs_recv,
    ag_send,
    ag_recv,
):
    me = lax.axis_index("tiles")
    comp = lax.axis_index("comp")
    place = ring_place(me, count)
    right = ring_tile(lax.rem(place + 1, count), count)
    left = ring_tile(lax.rem(place + count - 1, count), count)
    toward = (right, left)
    channels, cells = state_ref.shape
    rows = w_out_ref.shape[1]
    piece = rows // SUB
    half = cells // 2
    fields = lift_ref.shape[1]
    width = weights_ref.shape[-1]
    per_tile = cells // width
    block_cells = 256

    def chunk(offset):
        return lax.rem(place + offset + 2 * count, count)

    def peer(step):
        return lax.rem(me + step, count)

    def source(step):
        return lax.rem(me + count - step, count)

    barrier = pltpu.get_barrier_semaphore()
    for step in range(count):
        pl.semaphore_signal(
            barrier, inc=1, device_id={"tiles": peer(step), "comp": 1 - comp}, device_id_type=MESH
        )
        if step:
            pl.semaphore_signal(
                barrier, inc=1, device_id={"tiles": peer(step)}, device_id_type=MESH
            )
    pl.semaphore_wait(barrier, 2 * count - 1)

    pending = []

    def send(src, dst, send_sem, recv_sem, device):
        copy = pltpu.make_async_remote_copy(
            src_ref=src,
            dst_ref=dst,
            send_sem=send_sem,
            recv_sem=recv_sem,
            device_id=device,
            device_id_type=MESH,
        )
        copy.start()
        pending.append(copy)

    def arrived(dst, send_sem, recv_sem):
        pltpu.make_async_remote_copy(
            src_ref=dst,
            dst_ref=dst,
            send_sem=send_sem,
            recv_sem=recv_sem,
            device_id={"tiles": right},
            device_id_type=MESH,
        ).wait_recv()

    for step in range(count):
        send(
            partial_ref.at[peer(step)],
            force_recv.at[me],
            f_send.at[step],
            f_recv.at[step],
            {"tiles": peer(step), "comp": 1 - comp},
        )

    masked[...] = (cot_ref[...].astype(jnp.float32) * keep_ref[...]).astype(jnp.bfloat16)

    @pl.loop(0, count)
    def _(index):
        d_active[index] = jnp.dot(
            w_out_ref[index], masked[...], preferred_element_type=jnp.float32
        )

    for index in range(channels // 128):
        span = slice(index * 128, (index + 1) * 128)
        w_in_t[:, span] = w_in_ref[span, :].T

    for step in range(count):
        arrived(force_recv.at[source(step)], f_send.at[step], f_recv.at[step])
    total = force_recv[0].astype(jnp.float32)
    for index in range(1, count):
        total = total + force_recv[index].astype(jnp.float32)
    forcing[:, :half] = total[:fields]
    forcing[:, half:] = total[fields:]

    for start in range(0, cells, block_cells):
        span = slice(start, start + block_cells)
        summed_in = state_ref[:, span].astype(jnp.float32) + jnp.dot(
            lift_ref[...], forcing[:, span], precision=highest, preferred_element_type=jnp.float32
        )
        centre = summed_in - jnp.mean(summed_in, axis=0, keepdims=True)
        variance = jnp.mean(centre * centre, axis=0, keepdims=True)
        inverse = 1.0 / jnp.sqrt(variance + norm_eps)
        unit = centre * inverse
        inv_std[:, span] = inverse
        normed[:, span] = unit
        scaled[:, span] = (gain_ref[...] * unit).astype(jnp.bfloat16)

    def mlp(index):
        at = pl.multiple_of(index * rows, 16)
        w_rows = w_in_t[pl.ds(at, rows), :]
        for start in range(0, cells, block_cells):
            span = slice(start, start + block_cells)
            hidden = jnp.dot(w_rows, scaled[:, span], preferred_element_type=jnp.float32)
            gelu_value, gelu_slope = gelu_parts(hidden)
            act[:, span] = gelu_value.astype(jnp.bfloat16)
            d_hidden[index, :, span] = (d_active[index, :, span] * gelu_slope).astype(jnp.bfloat16)
        own[0, index] = lax.dot_general(
            act[...], masked[...], NT, preferred_element_type=jnp.float32
        )
        own[1, index] = lax.dot_general(
            d_hidden[index], scaled[...], NT, preferred_element_type=jnp.float32
        )

    signs = (-1, 1)

    def reduce_step(step):
        for sub in range(SUB):
            span = pl.ds(sub * piece, piece)
            for way in range(2):
                at = ring.at[way, step, span]
                arrived(at, rs_send.at[way, step, sub], rs_recv.at[way, step, sub])
                index = chunk(signs[way] * (step + 1))
                value = ring[way, step, span].astype(jnp.float32) + own[way, index, span]
                if step < count - 2:
                    ring[way, step, span] = value.astype(jnp.bfloat16)
                    send(
                        at,
                        ring.at[way, step + 1, span],
                        rs_send.at[way, step + 1, sub],
                        rs_recv.at[way, step + 1, sub],
                        {"tiles": toward[way]},
                    )
                else:
                    grads_ref[way, index, span] = value.astype(jnp.bfloat16)
                    gather_send(0, sub, way)

    def gather_send(step, sub, way):
        at = grads_ref.at[way, chunk(signs[way] * (step - 1)), pl.ds(sub * piece, piece)]
        send(
            at,
            at,
            ag_send.at[way, step, sub],
            ag_recv.at[way, step, sub],
            {"tiles": toward[way]},
        )

    def gather_step(step):
        for sub in range(SUB):
            for way in range(2):
                at = grads_ref.at[way, chunk(signs[way] * step), pl.ds(sub * piece, piece)]
                arrived(at, ag_send.at[way, step, sub], ag_recv.at[way, step, sub])
                if step < count - 2:
                    gather_send(step + 1, sub, way)

    mlp(place)
    for sub in range(SUB):
        span = pl.ds(sub * piece, piece)
        for way in range(2):
            first[way, span] = own[way, place, span].astype(jnp.bfloat16)
            send(
                first.at[way, span],
                ring.at[way, 0, span],
                rs_send.at[way, 0, sub],
                rs_recv.at[way, 0, sub],
                {"tiles": toward[way]},
            )
    for step in range(1, count // 2):

        @pl.loop(0, 2)
        def _(side):
            mlp(chunk(jnp.where(side == 0, -step, step)))

        reduce_step(step - 1)
    mlp(chunk(count // 2))
    reduce_step(count // 2 - 1)

    gain = gain_ref[...]
    for start in range(0, cells, block_cells):
        span = slice(start, start + block_cells)
        grad = jnp.dot(
            w_in_ref[...],
            d_hidden[:, :, span].reshape(count * rows, block_cells),
            preferred_element_type=jnp.float32,
        )
        unit = normed[:, span]
        weighted = grad * gain
        product = weighted * unit
        d_summed = inv_std[:, span] * (
            weighted
            - jnp.mean(weighted, axis=0, keepdims=True)
            - unit * jnp.mean(product, axis=0, keepdims=True)
        ) + masked[:, span].astype(jnp.float32)
        d_scaled[:, span] = grad * unit
        gs_ref[:, span] = d_summed
        lowered = jnp.dot(
            lift_t_ref[...], d_summed, precision=highest, preferred_element_type=jnp.float32
        )
        row = 0 if start < half else fields
        place_at = start % half
        lower[row : row + fields, place_at : place_at + block_cells] = lowered
        if start == block_cells:
            reduce_step(count // 2)
    df_send[...] = lower[...].astype(jnp.bfloat16)
    for step in range(count):
        send(
            df_send,
            df_recv.at[me],
            a_send.at[step],
            a_recv.at[step],
            {"tiles": peer(step), "comp": 1 - comp},
        )
    reduce_step(count // 2 + 1)
    small_send[0:8, :] = lax.dot_general(
        jnp.ones((8, cells), jnp.float32),
        d_scaled[...],
        NT,
        precision=highest,
        preferred_element_type=jnp.float32,
    )
    small_send[16:24, :] = lax.dot_general(
        forcing[...], gs_ref[...], NT, precision=highest, preferred_element_type=jnp.float32
    )
    reduce_step(count // 2 + 2)

    for step in range(count):
        arrived(df_recv.at[source(step)], a_send.at[step], a_recv.at[step])
    gather_step(0)
    half_blocks = per_tile // 2
    for index in range(count):
        landed = df_recv[index].astype(jnp.float32)
        for block in range(per_tile):
            row = block // half_blocks * fields
            column = block % half_blocks * width
            blocks[index * per_tile + block] = landed[row : row + fields, column : column + width]

    slots = weights_ref.shape[0]
    parts = 4
    sums = tuple(jnp.zeros((fields, width), jnp.float32) for _ in range(per_tile))
    for part in range(parts):

        def slot_body(slot, carry):
            force = blocks[spots_ref[slot]].astype(jnp.bfloat16)
            pulled = jnp.dot(force, weights_ref[slot], preferred_element_type=jnp.float32)
            return tuple(
                carry[block] + pulled * coef_ref[slot * per_tile + block]
                for block in range(per_tile)
            )

        span = slots // parts
        sums = lax.fori_loop(part * span, (part + 1) * span, slot_body, sums, unroll=4)
        if part < 2:
            gather_step(part + 1)
    d_exported = jnp.concatenate(sums, axis=1).astype(jnp.bfloat16)
    small_send[8:16, :] = lax.dot_general(
        d_exported, state_ref[...], NT, preferred_element_type=jnp.float32
    )
    for step in range(1, count):
        send(
            small_send,
            small_recv.at[me],
            s_send.at[step],
            s_recv.at[step],
            {"tiles": peer(step)},
        )
    gather_step(3)
    for start in range(0, cells, block_cells):
        span = slice(start, start + block_cells)
        gs_ref[:, span] += jnp.dot(
            export_t_ref[...], d_exported[:, span], preferred_element_type=jnp.float32
        )
    for step in range(4, count - 1):
        gather_step(step)
    small_recv[me] = small_send[...]
    for step in range(1, count):
        arrived(small_recv.at[source(step)], s_send.at[step], s_recv.at[step])
    total_small = small_recv[0]
    for index in range(1, count):
        total_small = total_small + small_recv[index]
    small_ref[...] = total_small
    for copy in pending:
        copy.wait_send()


def fused_body(
    state_field,
    cotangent,
    w_in,
    w_out,
    norm_gain,
    export_weight,
    lift_weight,
    wet_mask,
    remap_tile,
    source_block,
    target_block,
    slot_alive,
    remap_weights,
):
    count = lax.axis_size("tiles")
    state_local = state_field[0]
    weights_local = remap_weights[0]
    targets = remap_tile[0, :, 0]
    alive_local = slot_alive[0].astype(jnp.float32)
    channels, cells = state_local.shape
    hidden_size = w_in.shape[2]
    fields = export_weight.shape[1]
    width = weights_local.shape[-1]
    per_tile = cells // width
    slots = weights_local.shape[0]
    half = cells // 2
    rows = hidden_size // count
    exported = jnp.dot(
        export_weight[0], state_local, preferred_element_type=jnp.float32
    ).astype(jnp.bfloat16)
    pick_source = source_block[0][:, None] == jnp.arange(per_tile, dtype=jnp.int32)[None, :]
    source_rows = jnp.einsum(
        "lb,kbp->lkp",
        pick_source.astype(jnp.bfloat16),
        exported.reshape(fields, per_tile, width),
        preferred_element_type=jnp.float32,
    ).astype(jnp.bfloat16)
    products = jnp.einsum(
        "lkp,lqp->lkq", source_rows, weights_local, preferred_element_type=jnp.float32
    )
    spots = targets * per_tile + target_block[0]
    placing = jnp.where(
        spots[None, :] == jnp.arange(count * per_tile, dtype=jnp.int32)[:, None],
        alive_local[None, :],
        0.0,
    )
    dense = jnp.einsum("sl,lkq->skq", placing, products, precision=highest).astype(jnp.bfloat16)
    partial = (
        dense.reshape(count, 2, per_tile // 2, fields, width)
        .transpose(0, 1, 3, 2, 4)
        .reshape(count, 2 * fields, half)
    )
    coef = (pick_source.astype(jnp.float32) * alive_local[:, None]).reshape(slots * per_tile)
    is_ocean = lax.axis_index("comp") == 1
    keep = jnp.where(is_ocean, (wet_mask > 0).astype(jnp.float32), 1.0)[None, :]
    vmem = pl.BlockSpec(memory_space=pltpu.VMEM)
    smem = pl.BlockSpec(memory_space=pltpu.SMEM)
    steps = count - 1
    f32, b16 = jnp.float32, jnp.bfloat16
    dma = pltpu.SemaphoreType.DMA
    grads, small, grad_state = pl.pallas_call(
        functools.partial(fused_kernel, count),
        out_shape=(
            jax.ShapeDtypeStruct((2, count, rows, channels), b16),
            jax.ShapeDtypeStruct((24, channels), f32),
            jax.ShapeDtypeStruct((channels, cells), f32),
        ),
        in_specs=[smem] * 2 + [vmem] * 11,
        out_specs=(vmem,) * 3,
        scratch_shapes=[
            pltpu.VMEM((count, 2 * fields, half), b16),
            pltpu.VMEM((hidden_size, channels), b16),
            pltpu.VMEM((channels, cells), b16),
            pltpu.VMEM((count, rows, cells), f32),
            pltpu.VMEM((channels, cells), b16),
            pltpu.VMEM((channels, cells), f32),
            pltpu.VMEM((1, cells), f32),
            pltpu.VMEM((fields, cells), f32),
            pltpu.VMEM((rows, cells), b16),
            pltpu.VMEM((count, rows, cells), b16),
            pltpu.VMEM((channels, cells), f32),
            pltpu.VMEM((2, count, rows, channels), f32),
            pltpu.VMEM((2, rows, channels), b16),
            pltpu.VMEM((2, steps, rows, channels), b16),
            pltpu.VMEM((2 * fields, half), b16),
            pltpu.VMEM((count, 2 * fields, half), b16),
            pltpu.VMEM((2 * fields, half), f32),
            pltpu.VMEM((count * per_tile, fields, width), f32),
            pltpu.VMEM((24, channels), f32),
            pltpu.VMEM((count, 24, channels), f32),
            dma((count,)),
            dma((count,)),
            dma((count,)),
            dma((count,)),
            dma((count,)),
            dma((count,)),
            dma((2, steps, SUB)),
            dma((2, steps, SUB)),
            dma((2, steps, SUB)),
            dma((2, steps, SUB)),
        ],
        compiler_params=pltpu.CompilerParams(
            collective_id=0, has_side_effects=True, vmem_limit_bytes=52 * 1024 * 1024
        ),
    )(
        spots,
        coef,
        partial,
        state_local,
        cotangent[0],
        keep,
        w_in[0],
        w_out[0].reshape(count, rows, channels),
        norm_gain[0][:, None],
        lift_weight[0],
        lift_weight[0].T,
        export_weight[0].T,
        weights_local,
    )
    g_out = grads[0].reshape(hidden_size, channels).astype(f32)
    g_in = grads[1].reshape(hidden_size, channels).T.astype(f32)
    return (
        grad_state[None],
        g_in[None],
        g_out[None],
        small[0:1],
        small[8:16][None],
        small[16:24].T[None],
    )


def solution(mesh):
    placed = (
        P("comp", None, ("groups", "tiles")),
        P("comp", None, ("groups", "tiles")),
        P("comp", None, None),
        P("comp", None, None),
        P("comp", None),
        P("comp", None, None),
        P("comp", None, None),
        P(("groups", "tiles")),
        P("comp", "tiles", None),
        P("comp", "tiles"),
        P("comp", "tiles"),
        P("comp", "tiles"),
        P("comp", "tiles", None, None),
    )
    chosen = fused_body if mesh.shape["tiles"] == 8 else general_body
    return jax.shard_map(
        chosen,
        mesh=mesh,
        in_specs=placed,
        out_specs=(
            P("comp", None, ("groups", "tiles")),
            P(("groups", "comp"), None, None),
            P(("groups", "comp"), None, None),
            P(("groups", "comp"), None),
            P(("groups", "comp"), None, None),
            P(("groups", "comp"), None, None),
        ),
        check_vma=False,
    )
```
